256 devices in a mesh: ctx: 32 (over y, x, core), kvh: 8 (over z).
Axes of the slice: x: 4, y: 4, z: 8, core: 2. Of those that a mesh axis runs over, the one named last changes fastest.
Arguments:
- hidden_in: bfloat16 [4, 8192], P(None, 'ctx'), may hold values from -6 to 6
- w_query: bfloat16 [8192, 8192], P('ctx', 'kvh'), may hold values from -0.0625 to 0.0625
- key_cache: bfloat16 [768, 512, 1024], P('ctx', None, 'kvh')
- value_cache: bfloat16 [768, 512, 1024], P('ctx', None, 'kvh'), may hold values from -6 to 6
- chosen: int32 [4, 8, 16], P(None, 'kvh'), may hold values from 0 to 191, all different within a row
- owner_map: int32 [768], replicated, may hold values from 0 to 767, each once
- w_out: bfloat16 [8192, 8192], P('kvh', 'ctx'), may hold values from -0.75 to 0.75
Outputs:
- mixed: bfloat16 [4, 8192], P(None, ('ctx', 'kvh'))
The draws below stay inside these ranges and needn't reach their ends.
Inputs may be any that keep to these rules, and one draw needn't show every extreme that they name: `chosen`: distinct within a request and KV head. `owner_map`: A permutation; the block at storage position p lies on index p // 24 of ctx, in its slot p % 24.
All inputs are finite; a program needn't handle non-finite values.
Results may differ from the reference program's by a relative error of at most 0.012.
Values may be sent and summed in bfloat16 or wider, within the bound.
No kernel may reach another device: no remote copies, remote signals or barrier semaphores. Data moves between devices by JAX's collectives and lax.ppermute only.
A program may use at most 64 MiB of HBM per device.

```python
import jax
import jax.numpy as jnp
from jax import lax

D = 8192
KVH = 8
QPK = 8
HD = 128
BLOCK = 512
TOPB = 16
REQ = 4
NB = 768
NBLK = 192


def draw_key_cache(key, part):
    key = jax.random.fold_in(key, 11)
    first = jax.random.fold_in(key, 0)
    base = jax.random.normal(first, (NB, BLOCK, KVH * HD), jnp.float32) * 2.0
    base = jnp.clip(base, -12.0, 12.0)
    return base.astype(jnp.bfloat16)


def steps_of(key, extent, cuts, smallest, top_value):
    gain, own = 1.0, jax.random.fold_in(key, 6)
    for dim, shards_of in cuts:
        heights = jnp.exp(jax.random.uniform(jax.random.fold_in(own, dim), (shards_of,), jnp.float32, smallest / len(cuts), top_value / len(cuts)))
        gain = gain * jnp.repeat(heights, extent[dim] // shards_of).reshape([-1 if axis == dim else 1 for axis in range(len(extent))])
    return gain


def picks_of(key, rows, number_of, top, lift):
    sequence = jax.random.permutation(jax.random.fold_in(key, 1), number_of)
    boost = sequence
    for power in range(3):
        boost = boost * boost // number_of
    boost = boost * lift // number_of
    tickets = jax.random.randint(jax.random.fold_in(key, 2), (rows, number_of), 0, 4096) + boost
    fixed_rows = jax.random.permutation(jax.random.fold_in(key, 3), rows)[jnp.arange(number_of) % rows]
    tickets = jnp.where(jnp.arange(rows)[:, None] == fixed_rows[None, :], 1 << 14, tickets)
    priority = tickets * number_of + jnp.arange(number_of)
    return lax.top_k(priority.astype(jnp.int32), top)[1].astype(jnp.int32)


def centred(rng, dims, spread, most, cuts=(), held_as=jnp.bfloat16):
    result = spread * jax.random.normal(rng, dims, jnp.float32)
    if cuts:
        result = result * steps_of(rng, dims, cuts, -0.22, 0.18)
    return jnp.clip(result, -most, most).astype(held_as)


def setup_inputs(seed: int = 0) -> dict:
    seeds = jax.random.split(jax.random.key(seed), 8)
    hidden_in = centred(seeds[0], (REQ, D), 1.0, 6.0, ((1, 32),))
    w_query = centred(seeds[1], (D, KVH * QPK * HD), D ** -0.5, 0.0625, ((0, 32), (1, 8)))
    key_cache = draw_key_cache(jax.random.fold_in(seeds[7], 71), 0)
    value_cache = centred(seeds[3], (NB, BLOCK, KVH * HD), 1.0, 6.0, ((0, 32), (2, 8)))
    chosen = picks_of(seeds[4], REQ * KVH, NBLK, TOPB, 1365).reshape((REQ, KVH, TOPB))
    owner_map = jax.random.permutation(seeds[5], NB).astype(jnp.int32)
    w_out = centred(seeds[6], (KVH * QPK * HD, D), 0.125, 0.75, ((0, 8), (1, 32)))
    return {"hidden_in": hidden_in, "w_query": w_query, "key_cache": key_cache, "value_cache": value_cache, "chosen": chosen, "owner_map": owner_map, "w_out": w_out}


def block_partial(query_rows, key_block, value_block):
    scores = jnp.dot(query_rows, key_block.T, preferred_element_type=jnp.float32) / jnp.sqrt(jnp.float32(HD))
    peak = lax.optimization_barrier(jnp.max(scores, axis=-1))
    expo = jnp.exp(scores - peak[:, None])
    total = lax.optimization_barrier(jnp.sum(expo, axis=-1))
    weights = expo.astype(jnp.bfloat16)
    out = jnp.dot(weights, value_block, preferred_element_type=jnp.float32)
    return (peak, total, out)

def reference(hidden_in, w_query, key_cache, value_cache, chosen, owner_map, w_out):
    query = jnp.dot(hidden_in, w_query, preferred_element_type=jnp.float32).astype(jnp.bfloat16)
    query_heads = query.reshape(REQ, KVH, QPK, HD)
    glob = (jnp.arange(REQ, dtype=jnp.int32)[:, None, None] * NBLK + chosen).astype(jnp.int32)
    position = owner_map[glob]
    per_block = jax.vmap(jax.vmap(block_partial, in_axes=(None, 0, 0)), in_axes=(0, 0, 0))
    results = []
    for head in range(KVH):
        key_head = key_cache[:, :, head * HD:(head + 1) * HD]
        value_head = value_cache[:, :, head * HD:(head + 1) * HD]
        keys = key_head[position[:, head, :]]
        values = value_head[position[:, head, :]]
        peak, total, out = per_block(query_heads[:, head], keys, values)
        top = lax.optimization_barrier(jnp.max(peak, axis=1))
        factor = jnp.exp(peak - top[:, None, :])
        numer = lax.optimization_barrier(jnp.sum(factor[..., None] * out, axis=1))
        denom = lax.optimization_barrier(jnp.sum(factor * total, axis=1))
        results.append(numer / denom[..., None])
    attn = jnp.stack(results, axis=1).reshape(REQ, KVH * QPK * HD).astype(jnp.bfloat16)
    return jnp.dot(attn, w_out, preferred_element_type=jnp.float32).astype(jnp.bfloat16)
```

```python
import functools

import jax
import jax.numpy as jnp
from jax import lax
from jax.experimental import pallas as pl
from jax.experimental.pallas import tpu as pltpu
from jax.sharding import PartitionSpec as P

QPK = 8
HD = 128
NEG = -1e30
VMEM = pl.BlockSpec(memory_space=pltpu.VMEM)
SMEM = pl.BlockSpec(memory_space=pltpu.SMEM)
ANY = pl.BlockSpec(memory_space=pl.ANY)
HBM = pl.BlockSpec(memory_space=pltpu.HBM)
LIMIT = 24 * 1024 * 1024
GROUP = 4
AHEAD = 8
CTX_FIRST = 21
KVH_FIRST = 4


def in_hbm(array):
    return pltpu.with_memory_space_constraint(array, pltpu.HBM)


def query_kernel(
    hidden_ref, weight_ref, send_ref, keep_ref, hidden, weight, rows_ref, hidden_sem, weight_sem
):
    copies = (
        pltpu.make_async_copy(hidden_ref, hidden, hidden_sem),
        pltpu.make_async_copy(weight_ref, weight, weight_sem),
    )
    for copy in copies:
        copy.start()
    for copy in copies:
        copy.wait()
    part = jnp.dot(hidden[...], weight[...], preferred_element_type=jnp.float32)
    nreq = part.shape[0]
    for g in range(QPK):
        rows_ref[pl.ds(g, nreq, stride=QPK), :] = part[:, g * HD : (g + 1) * HD]
    half = keep_ref.shape[0]
    core = lax.rem(lax.axis_index("ctx"), 2)
    keep_ref[...] = rows_ref[pl.ds(pl.multiple_of(core * half, half), half), :]
    send_ref[...] = rows_ref[pl.ds(pl.multiple_of((1 - core) * half, half), half), :]


def spread_kernel(keep_ref, swapped_ref, out_ref):
    pair = keep_ref[...] + swapped_ref[...]
    for d in range(out_ref.shape[0]):
        out_ref[d] = pair


def fetch_kernel(
    chosen_ref, owner_ref, key_ref, value_ref, after_ref, key_buf, value_buf, items_ref,
    chosen, owner, sems, key_sem, value_sem,
):
    del after_ref
    slots_here = key_ref.shape[0]
    ahead = key_buf.shape[0]
    nreq, _, topb = chosen_ref.shape
    nblk = owner_ref.shape[0] // nreq
    last = items_ref.shape[0] - 1
    first = lax.axis_index("ctx") * slots_here
    tables = (
        pltpu.make_async_copy(chosen_ref, chosen, sems.at[0]),
        pltpu.make_async_copy(owner_ref, owner, sems.at[1]),
    )
    for copy in tables:
        copy.start()
    for copy in tables:
        copy.wait()

    def copies(place):
        slot = items_ref[slots_here + place]
        return (
            pltpu.make_async_copy(key_ref.at[slot], key_buf.at[place], key_sem.at[place]),
            pltpu.make_async_copy(value_ref.at[slot], value_buf.at[place], value_sem.at[place]),
        )

    for i in range(slots_here + GROUP):
        items_ref[i] = 0
    count = jnp.int32(0)
    for r in range(nreq):

        def look(j, count):
            slot = owner[r * nblk + chosen[r, 0, j]] - first
            here = (slot >= 0) & (slot < slots_here)

            @pl.when(here)
            def _():
                items_ref[count] = r
                items_ref[slots_here + count] = slot

            @pl.when(here & (count < ahead))
            def _():
                for copy in copies(count):
                    copy.start()

            return count + here.astype(jnp.int32)

        count = lax.fori_loop(0, topb, look, count, unroll=4)
    items_ref[last] = count

    def arrive(i, carry):
        for copy in copies(i):
            copy.wait()
        return carry

    lax.fori_loop(0, jnp.minimum(count, ahead), arrive, 0)


def attend_kernel(
    parts_ref, items_ref, key_ref, value_ref, key_all, value_all, out_ref,
    query_ref, top_ref, total_ref, acc_ref, key_late, value_late, key_sem, value_sem,
):
    slots_here = key_all.shape[0]
    ahead = key_ref.shape[0]
    count = items_ref[items_ref.shape[0] - 1]

    def copies(i):
        place, slot = i - ahead, items_ref[slots_here + i]
        return (
            pltpu.make_async_copy(key_all.at[slot], key_late.at[place], key_sem.at[place]),
            pltpu.make_async_copy(value_all.at[slot], value_late.at[place], value_sem.at[place]),
        )

    def bring(i, carry):
        for copy in copies(i):
            copy.start()
        return carry

    def arrive(i, carry):
        for copy in copies(i):
            copy.wait()
        return carry

    lax.fori_loop(ahead, count, bring, 0)
    half = parts_ref.shape[1]
    for side in range(2):
        query = parts_ref[1 - side]
        for d in range(side + 2, parts_ref.shape[0], 2):
            query = query + parts_ref[d]
        query_ref[side * half : (side + 1) * half, :] = query
    top_ref[...] = jnp.full(top_ref.shape, NEG, jnp.float32)
    total_ref[...] = jnp.zeros(total_ref.shape, jnp.float32)
    acc_ref[...] = jnp.zeros(acc_ref.shape, jnp.float32)

    def visit(step, keys, values, base):
        found = []
        for u in range(GROUP):
            place = step * GROUP + u
            i = base + place
            rows = pl.ds(pl.multiple_of(items_ref[i] * QPK, QPK), QPK)
            scores = lax.dot_general(
                query_ref[rows, :].astype(jnp.bfloat16), keys[place], (((1,), (1,)), ((), ())),
                preferred_element_type=jnp.float32,
            ) * (1.0 / HD**0.5)
            peak = jnp.max(scores, axis=1, keepdims=True)
            expo = jnp.exp(scores - peak)
            total = jnp.sum(expo, axis=1, keepdims=True)
            out = jnp.dot(
                expo.astype(jnp.bfloat16), values[place], preferred_element_type=jnp.float32
            )
            found.append((i < count, rows, peak, total, out))
        for here, rows, peak, total, out in found:
            peak = jnp.where(here, peak, NEG)
            old = top_ref[rows, :]
            new = jnp.maximum(old, peak)
            keep = jnp.exp(old - new)
            add = jnp.where(here, jnp.exp(peak - new), 0.0)
            top_ref[rows, :] = new
            total_ref[rows, :] = total_ref[rows, :] * keep + jnp.where(here, total, 0.0) * add
            acc_ref[rows, :] = acc_ref[rows, :] * keep + jnp.where(here, out, 0.0) * add

    for step in range(ahead // GROUP):

        @pl.when(step * GROUP < count)
        def _():
            visit(step, key_ref, value_ref, 0)

    lax.fori_loop(ahead, count, arrive, 0)

    def visit_late(step, carry):
        visit(step, key_late, value_late, ahead)
        return carry

    lax.fori_loop(0, jnp.maximum(count - ahead + GROUP - 1, 0) // GROUP, visit_late, 0)

    total = total_ref[...]
    some = total > 0.0
    safe = jnp.where(some, total, 1.0)
    mean = (acc_ref[...] / safe).astype(jnp.bfloat16)
    level = jnp.where(some, top_ref[...] + jnp.log(safe), NEG)
    high = level.astype(jnp.bfloat16).astype(jnp.float32)
    middle = (level - high).astype(jnp.bfloat16).astype(jnp.float32)
    low = level - high - middle
    nrow = level.shape[0]
    lane = lax.broadcasted_iota(jnp.int32, level.shape, 1)
    row = lax.broadcasted_iota(jnp.int32, level.shape, 0)
    packed = jnp.where(lane == row, high, 0.0)
    packed = jnp.where(lane == row + nrow, middle, packed)
    packed = jnp.where(lane == row + 2 * nrow, low, packed)
    packed = jnp.sum(packed, axis=0, keepdims=True)
    packed = jnp.broadcast_to(packed, (out_ref.shape[1] - nrow, HD)).astype(jnp.bfloat16)
    for d in range(out_ref.shape[0]):
        out_ref[d, :nrow, :] = mean
        out_ref[d, nrow:, :] = packed


def project_kernel(parts_ref, weight_ref, out_ref, level_ref, rows_ref):
    ndev = parts_ref.shape[0]
    nrow = rows_ref.shape[0]
    lane = lax.broadcasted_iota(jnp.int32, (nrow, HD), 1)
    row = lax.broadcasted_iota(jnp.int32, (nrow, HD), 0)
    mine = (lane == row) | (lane == row + nrow) | (lane == row + 2 * nrow)
    top = jnp.full((nrow, 1), NEG, jnp.float32)
    for d in range(ndev):
        packed = parts_ref[d, nrow:, :].astype(jnp.float32)[:1]
        level = jnp.sum(jnp.where(mine, packed, 0.0), axis=1, keepdims=True)
        level_ref[d] = jnp.broadcast_to(level, (nrow, HD))
        top = jnp.maximum(top, level)
    total = jnp.zeros((nrow, HD), jnp.float32)
    acc = jnp.zeros((nrow, HD), jnp.float32)
    for d in range(ndev):
        share = jnp.exp(level_ref[d] - top)
        total = total + share
        acc = acc + share * parts_ref[d, :nrow, :].astype(jnp.float32)
    rows_ref[...] = acc / total
    nreq = nrow // QPK
    term = jnp.zeros((nreq, weight_ref.shape[1]), jnp.float32)
    for g in range(QPK):
        heads = rows_ref[pl.ds(g, nreq, stride=QPK), :].astype(jnp.bfloat16)
        term = term + jnp.dot(
            heads, weight_ref[g * HD : (g + 1) * HD, :], preferred_element_type=jnp.float32
        )
    ndest = out_ref.shape[0]
    width = weight_ref.shape[1] // ndest
    for k in range(ndest):
        out_ref[(k - KVH_FIRST) % ndest, :, :width] = term[:, k * width : (k + 1) * width]


def sum_kernel(terms_ref, out_ref):
    out_ref[...] = jnp.sum(terms_ref[...], axis=0)[:, : out_ref.shape[1]].astype(out_ref.dtype)


def order(n, first):
    return [[first, first ^ 1] + [i for i in range(n) if i // 2 != first // 2]]


def turned(n, first):
    return [[(first + i) % n for i in range(n)]]


def local(nctx, nkvh, hidden_in, w_query, key_cache, value_cache, chosen, owner_map, w_out):
    nreq = hidden_in.shape[0]
    nrow = nreq * QPK
    slots_here, block, _ = key_cache.shape
    params = pltpu.CompilerParams(vmem_limit_bytes=LIMIT)
    state = pltpu.VMEM((nrow, HD), jnp.float32)
    half = jax.ShapeDtypeStruct((nrow // 2, HD), jnp.float32)
    send, keep = pl.pallas_call(
        query_kernel,
        out_shape=(half, half),
        in_specs=[HBM, HBM],
        out_specs=(VMEM, VMEM),
        scratch_shapes=[
            pltpu.VMEM(hidden_in.shape, hidden_in.dtype),
            pltpu.VMEM(w_query.shape, w_query.dtype),
            state,
            pltpu.SemaphoreType.DMA,
            pltpu.SemaphoreType.DMA,
        ],
        compiler_params=params,
        name="query",
    )(in_hbm(hidden_in), in_hbm(w_query))
    swapped = lax.ppermute(send, "ctx", [(i, i ^ 1) for i in range(nctx)])
    parts = pl.pallas_call(
        spread_kernel,
        out_shape=pltpu.VMEM((nctx, nrow // 2, HD), jnp.float32),
        in_specs=[VMEM, VMEM],
        out_specs=VMEM,
        compiler_params=params,
        name="spread",
    )(keep, swapped)
    every = lax.all_to_all(parts, "ctx", 0, 0, tiled=True, axis_index_groups=order(nctx, CTX_FIRST))
    blocks = pltpu.VMEM((AHEAD, block, HD), key_cache.dtype)
    late = slots_here - AHEAD
    keys, values, items = pl.pallas_call(
        fetch_kernel,
        out_shape=(blocks, blocks, jax.ShapeDtypeStruct((2 * slots_here + 8,), jnp.int32)),
        in_specs=[HBM, HBM, HBM, HBM, ANY],
        out_specs=(VMEM, VMEM, SMEM),
        scratch_shapes=[
            pltpu.SMEM(chosen.shape, jnp.int32),
            pltpu.SMEM(owner_map.shape, jnp.int32),
            pltpu.SemaphoreType.DMA((2,)),
            pltpu.SemaphoreType.DMA((AHEAD,)),
            pltpu.SemaphoreType.DMA((AHEAD,)),
        ],
        compiler_params=params,
        cost_estimate=pl.CostEstimate(flops=0, transcendentals=0, bytes_accessed=8 << 20),
        name="fetch",
    )(in_hbm(chosen), in_hbm(owner_map), in_hbm(key_cache), in_hbm(value_cache), swapped)
    means = pl.pallas_call(
        attend_kernel,
        out_shape=jax.ShapeDtypeStruct((nctx, nrow + 16, HD), jnp.bfloat16),
        in_specs=[VMEM, SMEM, VMEM, VMEM, HBM, HBM],
        out_specs=VMEM,
        scratch_shapes=[
            state, state, state, state,
            pltpu.VMEM((late, block, HD), key_cache.dtype),
            pltpu.VMEM((late, block, HD), key_cache.dtype),
            pltpu.SemaphoreType.DMA((late,)),
            pltpu.SemaphoreType.DMA((late,)),
        ],
        compiler_params=params,
        name="attend",
    )(every, items, keys, values, in_hbm(key_cache), in_hbm(value_cache))
    means = lax.all_to_all(means, "ctx", 0, 0, tiled=True, axis_index_groups=order(nctx, CTX_FIRST))
    terms = pl.pallas_call(
        project_kernel,
        out_shape=jax.ShapeDtypeStruct((nkvh, nreq, HD), jnp.float32),
        in_specs=[VMEM, VMEM],
        out_specs=VMEM,
        scratch_shapes=[pltpu.VMEM((nctx, nrow, HD), jnp.float32), state],
        compiler_params=params,
        name="project",
    )(means, w_out)
    terms = lax.all_to_all(terms, "kvh", 0, 0, tiled=True, axis_index_groups=turned(nkvh, KVH_FIRST))
    return pl.pallas_call(
        sum_kernel,
        out_shape=jax.ShapeDtypeStruct((nreq, w_out.shape[1] // nkvh), jnp.bfloat16),
        in_specs=[VMEM],
        out_specs=VMEM,
        compiler_params=params,
        name="sum",
    )(terms)


def solution(mesh):
    placed = (
        P(None, "ctx"),
        P("ctx", "kvh"),
        P("ctx", None, "kvh"),
        P("ctx", None, "kvh"),
        P(None, "kvh", None),
        P(),
        P("kvh", "ctx"),
    )
    return jax.shard_map(
        functools.partial(local, mesh.shape["ctx"], mesh.shape["kvh"]),
        mesh=mesh, in_specs=placed, out_specs=P(None, ("ctx", "kvh")), check_vma=False,
    )
```

```python
import functools

import jax
import jax.numpy as jnp
from jax import lax
from jax.experimental import pallas as pl
from jax.experimental.pallas import tpu as pltpu
from jax.sharding import PartitionSpec as P

QPK = 8
HD = 128
NEG = -1e30
VMEM = pl.BlockSpec(memory_space=pltpu.VMEM)
SMEM = pl.BlockSpec(memory_space=pltpu.SMEM)
HBM = pl.BlockSpec(memory_space=pltpu.HBM)
LIMIT = 24 * 1024 * 1024
GROUP = 4
AHEAD = 8
QSCALE = 256.0
STEP, STEPS = 12, 10
SPAN = 32
CTX_FIRST = 21
KVH_FIRST = 4
STRIPE_FIRST = (10, 14)


def in_hbm(array):
    return pltpu.with_memory_space_constraint(array, pltpu.HBM)


def find_items(chosen, owner, items, slots_here):
    nreq, _, topb = chosen.shape
    nblk = owner.shape[0] // nreq
    first = lax.axis_index("ctx") * slots_here
    for i in range(SPAN):
        items[i] = 0
    count = jnp.int32(0)
    for r in range(nreq):
        found = [owner[r * nblk + chosen[r, 0, j]] - first for j in range(topb)]
        for slot in found:
            items[count] = r
            items[SPAN + count] = slot
            count = count + ((slot >= 0) & (slot < slots_here)).astype(jnp.int32)
    items[2 * SPAN] = count


def query_kernel(
    slots_here, hidden_ref, weight_ref, chosen_ref, owner_ref, out_ref, items_ref,
    hidden, weight, chosen, owner, rows_ref, sems,
):
    tables = (
        pltpu.make_async_copy(chosen_ref, chosen, sems.at[0]),
        pltpu.make_async_copy(owner_ref, owner, sems.at[1]),
    )
    arrays = (
        pltpu.make_async_copy(hidden_ref, hidden, sems.at[2]),
        pltpu.make_async_copy(weight_ref, weight, sems.at[3]),
    )
    for copy in (*tables, *arrays):
        copy.start()
    for copy in tables:
        copy.wait()
    find_items(chosen, owner, items_ref, slots_here)
    for copy in arrays:
        copy.wait()
    part = jnp.dot(hidden[...], weight[...], preferred_element_type=jnp.float32)
    nreq = part.shape[0]
    for g in range(QPK):
        rows_ref[pl.ds(g, nreq, stride=QPK), :] = part[:, g * HD : (g + 1) * HD]
    out_ref[...] = rows_ref[...]


def fetch_kernel(items_ref, key_ref, value_ref, key_buf, value_buf, key_sem, value_sem):
    ahead = key_buf.shape[0]
    count = jnp.minimum(items_ref[2 * SPAN], ahead)

    def copies(place):
        slot = items_ref[SPAN + place]
        return (
            pltpu.make_async_copy(key_ref.at[slot], key_buf.at[place], key_sem.at[place]),
            pltpu.make_async_copy(value_ref.at[slot], value_buf.at[place], value_sem.at[place]),
        )

    def bring(i, carry):
        for copy in copies(i):
            copy.start()
        return carry

    def arrive(i, carry):
        for copy in copies(i):
            copy.wait()
        return carry

    lax.fori_loop(0, count, bring, 0)
    lax.fori_loop(0, count, arrive, 0)


def attend_kernel(
    query_ref, items_ref, key_ref, value_ref, key_all, value_all, out_ref,
    top_ref, total_ref, acc_ref, key_late, value_late, key_sem, value_sem,
):
    ahead = key_ref.shape[0]
    count = items_ref[2 * SPAN]

    def copies(i):
        place, slot = i - ahead, items_ref[SPAN + i]
        return (
            pltpu.make_async_copy(key_all.at[slot], key_late.at[place], key_sem.at[place]),
            pltpu.make_async_copy(value_all.at[slot], value_late.at[place], value_sem.at[place]),
        )

    def bring(i, carry):
        for copy in copies(i):
            copy.start()
        return carry

    def arrive(i, carry):
        for copy in copies(i):
            copy.wait()
        return carry

    lax.fori_loop(ahead, count, bring, 0)
    top_ref[...] = jnp.full(top_ref.shape, NEG, jnp.float32)
    total_ref[...] = jnp.zeros(total_ref.shape, jnp.float32)
    acc_ref[...] = jnp.zeros(acc_ref.shape, jnp.float32)

    def visit(step, keys, values, base, group):
        places = [step * group + u for u in range(group)]
        rows = [
            pl.ds(pl.multiple_of(items_ref[base + p] * QPK, QPK), QPK) for p in places
        ]
        scores = [
            lax.dot_general(
                query_ref[at, :].astype(jnp.bfloat16), keys[p], (((1,), (1,)), ((), ())),
                preferred_element_type=jnp.float32,
            ) * (1.0 / HD**0.5)
            for at, p in zip(rows, places)
        ]
        peaks = [jnp.max(x, axis=1, keepdims=True) for x in scores]
        expos = [jnp.exp(x - peak) for x, peak in zip(scores, peaks)]
        outs = [
            jnp.dot(x.astype(jnp.bfloat16), values[p], preferred_element_type=jnp.float32)
            for x, p in zip(expos, places)
        ]
        totals = [jnp.sum(x, axis=1, keepdims=True) for x in expos]
        found = [
            (base + p < count, *rest) for p, *rest in zip(places, rows, peaks, totals, outs)
        ]
        for here, rows, peak, total, out in found:
            peak = jnp.where(here, peak, NEG)
            old = top_ref[rows, :]
            new = jnp.maximum(old, peak)
            keep = jnp.exp(old - new)
            add = jnp.where(here, jnp.exp(peak - new), 0.0)
            top_ref[rows, :] = new
            total_ref[rows, :] = total_ref[rows, :] * keep + jnp.where(here, total, 0.0) * add
            acc_ref[rows, :] = acc_ref[rows, :] * keep + jnp.where(here, out, 0.0) * add

    @pl.when((count > 0) & (count <= GROUP))
    def _():
        visit(0, key_ref, value_ref, 0, GROUP)

    @pl.when(count > GROUP)
    def _():
        visit(0, key_ref, value_ref, 0, ahead)

    lax.fori_loop(ahead, count, arrive, 0)

    def visit_late(step, carry):
        visit(step, key_late, value_late, ahead, GROUP)
        return carry

    lax.fori_loop(0, jnp.maximum(count - ahead + GROUP - 1, 0) // GROUP, visit_late, 0)

    total = total_ref[...]
    some = total > 0.0
    safe = jnp.where(some, total, 1.0)
    out_ref[0] = acc_ref[...] / safe
    out_ref[1] = jnp.where(some, top_ref[...] + jnp.log(safe), NEG)


def join_kernel(own_ref, other_ref, out_ref):
    level_a, level_b = own_ref[1], other_ref[1]
    top = jnp.maximum(level_a, level_b)
    share_a, share_b = jnp.exp(level_a - top), jnp.exp(level_b - top)
    total = share_a + share_b
    mean = (share_a * own_ref[0] + share_b * other_ref[0]) / total
    level = top + jnp.log(total)
    most = jnp.max(jnp.max(jnp.abs(mean), axis=1, keepdims=True), axis=0, keepdims=True)
    ups = jnp.full((1, 1), 1.0, jnp.float32)
    downs = jnp.zeros(level.shape, jnp.float32)
    for i in range(STEPS):
        if i < STEPS - 1:
            ups = ups + jnp.where(most < 2.0 ** (3 - STEP * (i + 1)), 1.0, 0.0)
        downs = downs + jnp.where(jnp.abs(level) >= 2.0 ** (15 + STEP * i), 1.0, 0.0)
    mean = mean * scale_of(ups, STEP)
    level = level * scale_of(downs, -STEP)
    high = level.astype(jnp.bfloat16).astype(jnp.float32)
    middle = (level - high).astype(jnp.bfloat16).astype(jnp.float32)
    low = level - high - middle
    nrow = level.shape[0]
    lane = lax.broadcasted_iota(jnp.int32, level.shape, 1)
    row = lax.broadcasted_iota(jnp.int32, level.shape, 0)
    packed, counts = jnp.zeros(level.shape, jnp.float32), jnp.zeros(level.shape, jnp.float32)
    for i, part in enumerate((high, middle, low)):
        packed = jnp.where(lane == row + i * nrow, part, packed)
        counts = jnp.where(lane == row + i * nrow, downs, counts)
    packed = jnp.sum(packed, axis=0, keepdims=True)
    counts = jnp.sum(counts, axis=0, keepdims=True)
    out_ref[:nrow, :] = mean
    rest = (out_ref.shape[0] - nrow, HD)
    line = lax.broadcasted_iota(jnp.int32, rest, 0)
    out_ref[nrow:, :] = jnp.where(
        line == 0, packed, jnp.where(line == 1, counts, jnp.broadcast_to(ups, rest))
    )


def scale_of(count, step):
    scale = jnp.full(count.shape, 1.0, jnp.float32)
    for i in range(1, STEPS + 1):
        scale = jnp.where(count >= i, 2.0 ** (step * i), scale)
    return scale


def project_kernel(parts_ref, weight_ref, out_ref, rows_ref):
    ndev = parts_ref.shape[0]
    nrow = rows_ref.shape[0]
    lane = lax.broadcasted_iota(jnp.int32, (nrow, HD), 1)
    row = lax.broadcasted_iota(jnp.int32, (nrow, HD), 0)
    mine = (lane == row) | (lane == row + nrow) | (lane == row + 2 * nrow)
    levels, downs = [], []
    for d in range(ndev):
        rest = parts_ref[d, nrow:, :]
        packed = rest[0:1] * scale_of(rest[1:2], STEP)
        downs.append(scale_of(rest[2:3], -STEP))
        levels.append(jnp.sum(jnp.where(mine, packed, 0.0), axis=1, keepdims=True))
    top = functools.reduce(jnp.maximum, levels)
    total = jnp.zeros((nrow, 1), jnp.float32)
    acc = jnp.zeros((nrow, HD), jnp.float32)
    for d in range(ndev):
        share = jnp.exp(levels[d] - top)
        total = total + share
        acc = acc + share * (parts_ref[d, :nrow, :] * downs[d])
    rows_ref[...] = acc / total
    nreq = nrow // QPK
    term = jnp.zeros((nreq, weight_ref.shape[1]), jnp.float32)
    for g in range(QPK):
        heads = rows_ref[pl.ds(g, nreq, stride=QPK), :].astype(jnp.bfloat16)
        term = term + jnp.dot(
            heads, weight_ref[g * HD : (g + 1) * HD, :], preferred_element_type=jnp.float32
        )
    ndest = out_ref.shape[0]
    width = weight_ref.shape[1] // ndest
    for k in range(ndest):
        out_ref[(k - KVH_FIRST) % ndest, :, :width] = term[:, k * width : (k + 1) * width]


def planes(n, first):
    chips = [first // 2] + [i for i in range(n // 2) if i != first // 2]
    return [[2 * i + core for i in chips] for core in range(2)]


def stripes(n, firsts):
    groups = []
    for side, first in enumerate(firsts):
        chips = [first] + [i for i in range(n // 2) if i != first]
        groups.append([2 * i + (4 * i // n + side) % 2 for i in chips])
    return groups


def turned(n, first):
    return [[(first + i) % n for i in range(n)]]


def local(nctx, nkvh, hidden_in, w_query, key_cache, value_cache, chosen, owner_map, w_out):
    nreq = hidden_in.shape[0]
    nrow = nreq * QPK
    slots_here, block, _ = key_cache.shape
    params = pltpu.CompilerParams(vmem_limit_bytes=LIMIT)
    state = pltpu.VMEM((nrow, HD), jnp.float32)
    nchip = nctx // 2
    parts, items = pl.pallas_call(
        functools.partial(query_kernel, slots_here),
        out_shape=(
            jax.ShapeDtypeStruct((nrow, HD), jnp.float32),
            pltpu.SMEM((2 * SPAN + 8,), jnp.int32),
        ),
        in_specs=[HBM, HBM, HBM, HBM],
        out_specs=(VMEM, SMEM),
        scratch_shapes=[
            pltpu.VMEM(hidden_in.shape, hidden_in.dtype),
            pltpu.VMEM(w_query.shape, w_query.dtype),
            pltpu.SMEM(chosen.shape, jnp.int32),
            pltpu.SMEM(owner_map.shape, jnp.int32),
            state,
            pltpu.SemaphoreType.DMA((4,)),
        ],
        compiler_params=params,
        name="query",
    )(in_hbm(hidden_in), in_hbm(w_query), in_hbm(chosen), in_hbm(owner_map))
    swap = [(i, i ^ 1) for i in range(nctx)]
    other = lax.ppermute(parts, "ctx", swap)
    blocks = pltpu.VMEM((AHEAD, block, HD), key_cache.dtype)
    late = slots_here - AHEAD
    assert slots_here < SPAN
    keys, values = pl.pallas_call(
        fetch_kernel,
        out_shape=(blocks, blocks),
        in_specs=[SMEM, HBM, HBM],
        out_specs=(VMEM, VMEM),
        scratch_shapes=[
            pltpu.SemaphoreType.DMA((AHEAD,)),
            pltpu.SemaphoreType.DMA((AHEAD,)),
        ],
        compiler_params=params,
        cost_estimate=pl.CostEstimate(flops=0, transcendentals=0, bytes_accessed=4 << 20),
        name="fetch",
    )(items, in_hbm(key_cache), in_hbm(value_cache))
    other, keys, values = lax.optimization_barrier((other, keys, values))
    pair = ((parts + other) * QSCALE).astype(jnp.float16)
    every = jnp.broadcast_to(pair[None], (nchip, nrow, HD))
    every = lax.all_to_all(every, "ctx", 0, 0, tiled=True, axis_index_groups=stripes(nctx, STRIPE_FIRST))
    query = jnp.sum(every.astype(jnp.float32), axis=0) * (1.0 / QSCALE)
    states = pl.pallas_call(
        attend_kernel,
        out_shape=jax.ShapeDtypeStruct((2, nrow, HD), jnp.float32),
        in_specs=[VMEM, SMEM, VMEM, VMEM, HBM, HBM],
        out_specs=VMEM,
        scratch_shapes=[
            state, state, state,
            pltpu.VMEM((late, block, HD), key_cache.dtype),
            pltpu.VMEM((late, block, HD), key_cache.dtype),
            pltpu.SemaphoreType.DMA((late,)),
            pltpu.SemaphoreType.DMA((late,)),
        ],
        compiler_params=params,
        name="attend",
    )(query, items, keys, values, in_hbm(key_cache), in_hbm(value_cache))
    others = lax.ppermute(states, "ctx", swap)
    means = pl.pallas_call(
        join_kernel,
        out_shape=jax.ShapeDtypeStruct((nrow + 8, HD), jnp.float32),
        in_specs=[VMEM, VMEM],
        out_specs=VMEM,
        compiler_params=params,
        name="join",
    )(states, others)
    means = jnp.broadcast_to(means.astype(jnp.float16)[None], (nchip, *means.shape))
    means = lax.all_to_all(means, "ctx", 0, 0, tiled=True, axis_index_groups=planes(nctx, CTX_FIRST))
    means = means.astype(jnp.float32)
    terms = pl.pallas_call(
        project_kernel,
        out_shape=jax.ShapeDtypeStruct((nkvh, nreq, HD), jnp.float32),
        in_specs=[VMEM, VMEM],
        out_specs=VMEM,
        scratch_shapes=[state],
        compiler_params=params,
        name="project",
    )(means, w_out)
    terms = lax.all_to_all(terms, "kvh", 0, 0, tiled=True, axis_index_groups=turned(nkvh, KVH_FIRST))
    return jnp.sum(terms, axis=0)[:, : w_out.shape[1] // nkvh].astype(jnp.bfloat16)


def solution(mesh):
    placed = (
        P(None, "ctx"),
        P("ctx", "kvh"),
        P("ctx", None, "kvh"),
        P("ctx", None, "kvh"),
        P(None, "kvh", None),
        P(),
        P("kvh", "ctx"),
    )
    return jax.shard_map(
        functools.partial(local, mesh.shape["ctx"], mesh.shape["kvh"]),
        mesh=mesh, in_specs=placed, out_specs=P(None, ("ctx", "kvh")), check_vma=False,
    )
```

```python
import functools

import jax
import jax.numpy as jnp
from jax import lax
from jax.experimental import pallas as pl
from jax.experimental.pallas import tpu as pltpu
from jax.sharding import PartitionSpec as P

QPK = 8
HD = 128
NEG = -1e30
VMEM = pl.BlockSpec(memory_space=pltpu.VMEM)
SMEM = pl.BlockSpec(memory_space=pltpu.SMEM)
HBM = pl.BlockSpec(memory_space=pltpu.HBM)
LIMIT = 24 * 1024 * 1024
GROUP = 4
AHEAD = 8
QSCALE = 256.0
STEP, STEPS = 12, 10
SPAN = 32
CTX_FIRST = 21
KVH_FIRST = 4
STRIPE_FIRST = (10, 14)


def in_hbm(array):
    return pltpu.with_memory_space_constraint(array, pltpu.HBM)


def find_items(chosen, owner, items, slots_here):
    nreq, _, topb = chosen.shape
    nblk = owner.shape[0] // nreq
    first = lax.axis_index("ctx") * slots_here
    for i in range(SPAN):
        items[i] = 0
    count = jnp.int32(0)
    for r in range(nreq):
        found = [owner[r * nblk + chosen[r, 0, j]] - first for j in range(topb)]
        for slot in found:
            items[count] = r
            items[SPAN + count] = slot
            count = count + ((slot >= 0) & (slot < slots_here)).astype(jnp.int32)
    items[2 * SPAN] = count


def query_kernel(
    slots_here, hidden_ref, weight_ref, chosen_ref, owner_ref, out_ref, items_ref,
    hidden, weight, chosen, owner, rows_ref, sems,
):
    tables = (
        pltpu.make_async_copy(chosen_ref, chosen, sems.at[0]),
        pltpu.make_async_copy(owner_ref, owner, sems.at[1]),
    )
    arrays = (
        pltpu.make_async_copy(hidden_ref, hidden, sems.at[2]),
        pltpu.make_async_copy(weight_ref, weight, sems.at[3]),
    )
    for copy in (*tables, *arrays):
        copy.start()
    for copy in tables:
        copy.wait()
    find_items(chosen, owner, items_ref, slots_here)
    for copy in arrays:
        copy.wait()
    part = jnp.dot(hidden[...], weight[...], preferred_element_type=jnp.float32)
    nreq = part.shape[0]
    for g in range(QPK):
        rows_ref[pl.ds(g, nreq, stride=QPK), :] = part[:, g * HD : (g + 1) * HD]
    out_ref[...] = rows_ref[...]


def fetch_kernel(items_ref, key_ref, value_ref, key_buf, value_buf, key_sem, value_sem):
    ahead = key_buf.shape[0]
    count = jnp.minimum(items_ref[2 * SPAN], ahead)

    def copies(place):
        slot = items_ref[SPAN + place]
        return (
            pltpu.make_async_copy(key_ref.at[slot], key_buf.at[place], key_sem.at[place]),
            pltpu.make_async_copy(value_ref.at[slot], value_buf.at[place], value_sem.at[place]),
        )

    def bring(i, carry):
        for copy in copies(i):
            copy.start()
        return carry

    def arrive(i, carry):
        for copy in copies(i):
            copy.wait()
        return carry

    lax.fori_loop(0, count, bring, 0)
    lax.fori_loop(0, count, arrive, 0)


def attend_kernel(
    query_ref, items_ref, key_ref, value_ref, key_all, value_all, out_ref,
    top_ref, total_ref, acc_ref, key_late, value_late, key_sem, value_sem,
):
    ahead = key_ref.shape[0]
    count = items_ref[2 * SPAN]

    def copies(i):
        place, slot = i - ahead, items_ref[SPAN + i]
        return (
            pltpu.make_async_copy(key_all.at[slot], key_late.at[place], key_sem.at[place]),
            pltpu.make_async_copy(value_all.at[slot], value_late.at[place], value_sem.at[place]),
        )

    def bring(i, carry):
        for copy in copies(i):
            copy.start()
        return carry

    def arrive(i, carry):
        for copy in copies(i):
            copy.wait()
        return carry

    lax.fori_loop(ahead, count, bring, 0)
    top_ref[...] = jnp.full(top_ref.shape, NEG, jnp.float32)
    total_ref[...] = jnp.zeros(total_ref.shape, jnp.float32)
    acc_ref[...] = jnp.zeros(acc_ref.shape, jnp.float32)

    def visit(step, keys, values, base, group):
        places = [step * group + u for u in range(group)]
        rows = [
            pl.ds(pl.multiple_of(items_ref[base + p] * QPK, QPK), QPK) for p in places
        ]
        scores = [
            lax.dot_general(
                query_ref[at, :].astype(jnp.bfloat16), keys[p], (((1,), (1,)), ((), ())),
                preferred_element_type=jnp.float32,
            ) * (1.0 / HD**0.5)
            for at, p in zip(rows, places)
        ]
        peaks = [jnp.max(x, axis=1, keepdims=True) for x in scores]
        expos = [jnp.exp(x - peak) for x, peak in zip(scores, peaks)]
        highs = [x.astype(jnp.bfloat16) for x in expos]
        lows = [(x - h.astype(jnp.float32)).astype(jnp.bfloat16) for x, h in zip(expos, highs)]
        outs = [
            jnp.dot(
                jnp.concatenate([h, w], axis=0), values[p], preferred_element_type=jnp.float32
            )
            for h, w, p in zip(highs, lows, places)
        ]
        outs = [x[:QPK] + x[QPK:] for x in outs]
        totals = [jnp.sum(x, axis=1, keepdims=True) for x in expos]
        found = [
            (base + p < count, *rest) for p, *rest in zip(places, rows, peaks, totals, outs)
        ]
        for here, rows, peak, total, out in found:
            peak = jnp.where(here, peak, NEG)
            old = top_ref[rows, :]
            new = jnp.maximum(old, peak)
            keep = jnp.exp(old - new)
            add = jnp.where(here, jnp.exp(peak - new), 0.0)
            top_ref[rows, :] = new
            total_ref[rows, :] = total_ref[rows, :] * keep + jnp.where(here, total, 0.0) * add
            acc_ref[rows, :] = acc_ref[rows, :] * keep + jnp.where(here, out, 0.0) * add

    @pl.when((count > 0) & (count <= GROUP))
    def _():
        visit(0, key_ref, value_ref, 0, GROUP)

    @pl.when(count > GROUP)
    def _():
        visit(0, key_ref, value_ref, 0, ahead)

    lax.fori_loop(ahead, count, arrive, 0)

    def visit_late(step, carry):
        visit(step, key_late, value_late, ahead, GROUP)
        return carry

    lax.fori_loop(0, jnp.maximum(count - ahead + GROUP - 1, 0) // GROUP, visit_late, 0)

    total = total_ref[...]
    some = total > 0.0
    safe = jnp.where(some, total, 1.0)
    out_ref[0] = acc_ref[...] / safe
    out_ref[1] = jnp.where(some, top_ref[...] + jnp.log(safe), NEG)


def join_kernel(own_ref, other_ref, out_ref):
    level_a, level_b = own_ref[1], other_ref[1]
    top = jnp.maximum(level_a, level_b)
    share_a, share_b = jnp.exp(level_a - top), jnp.exp(level_b - top)
    total = share_a + share_b
    mean = (share_a * own_ref[0] + share_b * other_ref[0]) / total
    level = top + jnp.log(total)
    most = jnp.max(jnp.max(jnp.abs(mean), axis=1, keepdims=True), axis=0, keepdims=True)
    ups = jnp.full((1, 1), 1.0, jnp.float32)
    downs = jnp.zeros(level.shape, jnp.float32)
    for i in range(STEPS):
        if i < STEPS - 1:
            ups = ups + jnp.where(most < 2.0 ** (3 - STEP * (i + 1)), 1.0, 0.0)
        downs = downs + jnp.where(jnp.abs(level) >= 2.0 ** (15 + STEP * i), 1.0, 0.0)
    mean = mean * scale_of(ups, STEP)
    level = level * scale_of(downs, -STEP)
    high = level.astype(jnp.bfloat16).astype(jnp.float32)
    middle = (level - high).astype(jnp.bfloat16).astype(jnp.float32)
    low = level - high - middle
    nrow = level.shape[0]
    lane = lax.broadcasted_iota(jnp.int32, level.shape, 1)
    row = lax.broadcasted_iota(jnp.int32, level.shape, 0)
    packed, counts = jnp.zeros(level.shape, jnp.float32), jnp.zeros(level.shape, jnp.float32)
    for i, part in enumerate((high, middle, low)):
        packed = jnp.where(lane == row + i * nrow, part, packed)
        counts = jnp.where(lane == row + i * nrow, downs, counts)
    packed = jnp.sum(packed, axis=0, keepdims=True)
    counts = jnp.sum(counts, axis=0, keepdims=True)
    out_ref[:nrow, :] = mean
    rest = (out_ref.shape[0] - nrow, HD)
    line = lax.broadcasted_iota(jnp.int32, rest, 0)
    out_ref[nrow:, :] = jnp.where(
        line == 0, packed, jnp.where(line == 1, counts, jnp.broadcast_to(ups, rest))
    )


def scale_of(count, step):
    scale = jnp.full(count.shape, 1.0, jnp.float32)
    for i in range(1, STEPS + 1):
        scale = jnp.where(count >= i, 2.0 ** (step * i), scale)
    return scale


def project_kernel(parts_ref, weight_ref, out_ref, rows_ref):
    ndev = parts_ref.shape[0]
    nrow = rows_ref.shape[0]
    lane = lax.broadcasted_iota(jnp.int32, (nrow, HD), 1)
    row = lax.broadcasted_iota(jnp.int32, (nrow, HD), 0)
    mine = (lane == row) | (lane == row + nrow) | (lane == row + 2 * nrow)
    levels, downs = [], []
    for d in range(ndev):
        rest = parts_ref[d, nrow:, :]
        packed = rest[0:1] * scale_of(rest[1:2], STEP)
        downs.append(scale_of(rest[2:3], -STEP))
        levels.append(jnp.sum(jnp.where(mine, packed, 0.0), axis=1, keepdims=True))
    top = functools.reduce(jnp.maximum, levels)
    total = jnp.zeros((nrow, 1), jnp.float32)
    acc = jnp.zeros((nrow, HD), jnp.float32)
    for d in range(ndev):
        share = jnp.exp(levels[d] - top)
        total = total + share
        acc = acc + share * (parts_ref[d, :nrow, :] * downs[d])
    rows_ref[...] = acc / total
    nreq = nrow // QPK
    term = jnp.zeros((nreq, weight_ref.shape[1]), jnp.float32)
    for g in range(QPK):
        heads = rows_ref[pl.ds(g, nreq, stride=QPK), :].astype(jnp.bfloat16)
        term = term + jnp.dot(
            heads, weight_ref[g * HD : (g + 1) * HD, :], preferred_element_type=jnp.float32
        )
    ndest = out_ref.shape[0]
    width = weight_ref.shape[1] // ndest
    for k in range(ndest):
        out_ref[(k - KVH_FIRST) % ndest, :, :width] = term[:, k * width : (k + 1) * width]


def planes(n, first):
    chips = [first // 2] + [i for i in range(n // 2) if i != first // 2]
    return [[2 * i + core for i in chips] for core in range(2)]


def stripes(n, firsts):
    groups = []
    for side, first in enumerate(firsts):
        chips = [first] + [i for i in range(n // 2) if i != first]
        groups.append([2 * i + (4 * i // n + side) % 2 for i in chips])
    return groups


def turned(n, first):
    return [[(first + i) % n for i in range(n)]]


def local(nctx, nkvh, hidden_in, w_query, key_cache, value_cache, chosen, owner_map, w_out):
    nreq = hidden_in.shape[0]
    nrow = nreq * QPK
    slots_here, block, _ = key_cache.shape
    params = pltpu.CompilerParams(vmem_limit_bytes=LIMIT)
    state = pltpu.VMEM((nrow, HD), jnp.float32)
    nchip = nctx // 2
    parts, items = pl.pallas_call(
        functools.partial(query_kernel, slots_here),
        out_shape=(
            jax.ShapeDtypeStruct((nrow, HD), jnp.float32),
            pltpu.SMEM((2 * SPAN + 8,), jnp.int32),
        ),
        in_specs=[HBM, HBM, HBM, HBM],
        out_specs=(VMEM, SMEM),
        scratch_shapes=[
            pltpu.VMEM(hidden_in.shape, hidden_in.dtype),
            pltpu.VMEM(w_query.shape, w_query.dtype),
            pltpu.SMEM(chosen.shape, jnp.int32),
            pltpu.SMEM(owner_map.shape, jnp.int32),
            state,
            pltpu.SemaphoreType.DMA((4,)),
        ],
        compiler_params=params,
        name="query",
    )(in_hbm(hidden_in), in_hbm(w_query), in_hbm(chosen), in_hbm(owner_map))
    swap = [(i, i ^ 1) for i in range(nctx)]
    other = lax.ppermute(parts, "ctx", swap)
    blocks = pltpu.VMEM((AHEAD, block, HD), key_cache.dtype)
    late = slots_here - AHEAD
    assert slots_here < SPAN
    keys, values = pl.pallas_call(
        fetch_kernel,
        out_shape=(blocks, blocks),
        in_specs=[SMEM, HBM, HBM],
        out_specs=(VMEM, VMEM),
        scratch_shapes=[
            pltpu.SemaphoreType.DMA((AHEAD,)),
            pltpu.SemaphoreType.DMA((AHEAD,)),
        ],
        compiler_params=params,
        cost_estimate=pl.CostEstimate(flops=0, transcendentals=0, bytes_accessed=4 << 20),
        name="fetch",
    )(items, in_hbm(key_cache), in_hbm(value_cache))
    other, keys, values = lax.optimization_barrier((other, keys, values))
    pair = ((parts + other) * QSCALE).astype(jnp.float16)
    every = jnp.broadcast_to(pair[None], (nchip, nrow, HD))
    every = lax.all_to_all(every, "ctx", 0, 0, tiled=True, axis_index_groups=stripes(nctx, STRIPE_FIRST))
    query = jnp.sum(every.astype(jnp.float32), axis=0) * (1.0 / QSCALE)
    states = pl.pallas_call(
        attend_kernel,
        out_shape=jax.ShapeDtypeStruct((2, nrow, HD), jnp.float32),
        in_specs=[VMEM, SMEM, VMEM, VMEM, HBM, HBM],
        out_specs=VMEM,
        scratch_shapes=[
            state, state, state,
            pltpu.VMEM((late, block, HD), key_cache.dtype),
            pltpu.VMEM((late, block, HD), key_cache.dtype),
            pltpu.SemaphoreType.DMA((late,)),
            pltpu.SemaphoreType.DMA((late,)),
        ],
        compiler_params=params,
        name="attend",
    )(query, items, keys, values, in_hbm(key_cache), in_hbm(value_cache))
    others = lax.ppermute(states, "ctx", swap)
    means = pl.pallas_call(
        join_kernel,
        out_shape=jax.ShapeDtypeStruct((nrow + 8, HD), jnp.float32),
        in_specs=[VMEM, VMEM],
        out_specs=VMEM,
        compiler_params=params,
        name="join",
    )(states, others)
    means = jnp.broadcast_to(means.astype(jnp.float16)[None], (nchip, *means.shape))
    means = lax.all_to_all(means, "ctx", 0, 0, tiled=True, axis_index_groups=planes(nctx, CTX_FIRST))
    means = means.astype(jnp.float32)
    terms = pl.pallas_call(
        project_kernel,
        out_shape=jax.ShapeDtypeStruct((nkvh, nreq, HD), jnp.float32),
        in_specs=[VMEM, VMEM],
        out_specs=VMEM,
        scratch_shapes=[state],
        compiler_params=params,
        name="project",
    )(means, w_out)
    terms = lax.all_to_all(terms, "kvh", 0, 0, tiled=True, axis_index_groups=turned(nkvh, KVH_FIRST))
    return jnp.sum(terms, axis=0)[:, : w_out.shape[1] // nkvh].astype(jnp.bfloat16)


def solution(mesh):
    placed = (
        P(None, "ctx"),
        P("ctx", "kvh"),
        P("ctx", None, "kvh"),
        P("ctx", None, "kvh"),
        P(None, "kvh", None),
        P(),
        P("kvh", "ctx"),
    )
    return jax.shard_map(
        functools.partial(local, mesh.shape["ctx"], mesh.shape["kvh"]),
        mesh=mesh, in_specs=placed, out_specs=P(None, ("ctx", "kvh")), check_vma=False,
    )
```

```python
import functools

import jax
import jax.numpy as jnp
from jax import lax
from jax.experimental import pallas as pl
from jax.experimental.pallas import tpu as pltpu
from jax.sharding import PartitionSpec as P

QPK = 8
HD = 128
NEG = -1e30
VMEM = pl.BlockSpec(memory_space=pltpu.VMEM)
SMEM = pl.BlockSpec(memory_space=pltpu.SMEM)
HBM = pl.BlockSpec(memory_space=pltpu.HBM)
LIMIT = 24 * 1024 * 1024
GROUP = 4
AHEAD = 8
QSCALE = 256.0
STEP, STEPS = 12, 10
SPAN = 32
CTX_FIRST = 21
KVH_FIRST = 5
STRIPE_FIRST = (10, 14)


def in_hbm(array):
    return pltpu.with_memory_space_constraint(array, pltpu.HBM)


def find_items(chosen, owner, items, slots_here):
    nreq, _, topb = chosen.shape
    nblk = owner.shape[0] // nreq
    first = lax.axis_index("ctx") * slots_here
    for i in range(SPAN):
        items[i] = 0
    count = jnp.int32(0)
    for r in range(nreq):
        found = [owner[r * nblk + chosen[r, 0, j]] - first for j in range(topb)]
        for slot in found:
            items[count] = r
            items[SPAN + count] = slot
            count = count + ((slot >= 0) & (slot < slots_here)).astype(jnp.int32)
    items[2 * SPAN] = count


def query_kernel(
    slots_here, hidden_ref, weight_ref, chosen_ref, owner_ref, out_ref, items_ref,
    hidden, weight, chosen, owner, rows_ref, sems,
):
    tables = (
        pltpu.make_async_copy(chosen_ref, chosen, sems.at[0]),
        pltpu.make_async_copy(owner_ref, owner, sems.at[1]),
    )
    arrays = (
        pltpu.make_async_copy(hidden_ref, hidden, sems.at[2]),
        pltpu.make_async_copy(weight_ref, weight, sems.at[3]),
    )
    for copy in (*tables, *arrays):
        copy.start()
    for copy in tables:
        copy.wait()
    find_items(chosen, owner, items_ref, slots_here)
    for copy in arrays:
        copy.wait()
    part = jnp.dot(hidden[...], weight[...], preferred_element_type=jnp.float32)
    nreq = part.shape[0]
    for g in range(QPK):
        rows_ref[pl.ds(g, nreq, stride=QPK), :] = part[:, g * HD : (g + 1) * HD]
    out_ref[...] = rows_ref[...]


def fetch_kernel(items_ref, key_ref, value_ref, key_buf, value_buf, key_sem, value_sem):
    ahead = key_buf.shape[0]
    count = jnp.minimum(items_ref[2 * SPAN], ahead)

    def copies(place):
        slot = items_ref[SPAN + place]
        return (
            pltpu.make_async_copy(key_ref.at[slot], key_buf.at[place], key_sem.at[place]),
            pltpu.make_async_copy(value_ref.at[slot], value_buf.at[place], value_sem.at[place]),
        )

    def bring(i, carry):
        for copy in copies(i):
            copy.start()
        return carry

    def arrive(i, carry):
        for copy in copies(i):
            copy.wait()
        return carry

    lax.fori_loop(0, count, bring, 0)
    lax.fori_loop(0, count, arrive, 0)


def attend_kernel(
    query_ref, items_ref, key_ref, value_ref, key_all, value_all, out_ref,
    top_ref, total_ref, acc_ref, key_late, value_late, key_sem, value_sem,
):
    ahead = key_ref.shape[0]
    count = items_ref[2 * SPAN]

    def copies(i):
        place, slot = i - ahead, items_ref[SPAN + i]
        return (
            pltpu.make_async_copy(key_all.at[slot], key_late.at[place], key_sem.at[place]),
            pltpu.make_async_copy(value_all.at[slot], value_late.at[place], value_sem.at[place]),
        )

    def bring(i, carry):
        for copy in copies(i):
            copy.start()
        return carry

    def arrive(i, carry):
        for copy in copies(i):
            copy.wait()
        return carry

    lax.fori_loop(ahead, count, bring, 0)
    top_ref[...] = jnp.full(top_ref.shape, NEG, jnp.float32)
    total_ref[...] = jnp.zeros(total_ref.shape, jnp.float32)
    acc_ref[...] = jnp.zeros(acc_ref.shape, jnp.float32)

    def visit(step, keys, values, base, group):
        places = [step * group + u for u in range(group)]
        rows = [
            pl.ds(pl.multiple_of(items_ref[base + p] * QPK, QPK), QPK) for p in places
        ]
        scores = [
            lax.dot_general(
                query_ref[at, :].astype(jnp.bfloat16), keys[p], (((1,), (1,)), ((), ())),
                preferred_element_type=jnp.float32,
            ) * (1.0 / HD**0.5)
            for at, p in zip(rows, places)
        ]
        peaks = [jnp.max(x, axis=1, keepdims=True) for x in scores]
        expos = [jnp.exp(x - peak) for x, peak in zip(scores, peaks)]
        outs = [
            jnp.dot(x.astype(jnp.bfloat16), values[p], preferred_element_type=jnp.float32)
            for x, p in zip(expos, places)
        ]
        totals = [jnp.sum(x, axis=1, keepdims=True) for x in expos]
        found = [
            (base + p < count, *rest) for p, *rest in zip(places, rows, peaks, totals, outs)
        ]
        for here, rows, peak, total, out in found:
            peak = jnp.where(here, peak, NEG)
            old = top_ref[rows, :]
            new = jnp.maximum(old, peak)
            keep = jnp.exp(old - new)
            add = jnp.where(here, jnp.exp(peak - new), 0.0)
            top_ref[rows, :] = new
            total_ref[rows, :] = total_ref[rows, :] * keep + jnp.where(here, total, 0.0) * add
            acc_ref[rows, :] = acc_ref[rows, :] * keep + jnp.where(here, out, 0.0) * add

    @pl.when((count > 0) & (count <= GROUP))
    def _():
        visit(0, key_ref, value_ref, 0, GROUP)

    @pl.when(count > GROUP)
    def _():
        visit(0, key_ref, value_ref, 0, ahead)

    lax.fori_loop(ahead, count, arrive, 0)

    def visit_late(step, carry):
        visit(step, key_late, value_late, ahead, GROUP)
        return carry

    lax.fori_loop(0, jnp.maximum(count - ahead + GROUP - 1, 0) // GROUP, visit_late, 0)

    total = total_ref[...]
    some = total > 0.0
    safe = jnp.where(some, total, 1.0)
    out_ref[0] = acc_ref[...] / safe
    out_ref[1] = jnp.where(some, top_ref[...] + jnp.log(safe), NEG)


def join_kernel(own_ref, other_ref, out_ref):
    level_a, level_b = own_ref[1], other_ref[1]
    top = jnp.maximum(level_a, level_b)
    share_a, share_b = jnp.exp(level_a - top), jnp.exp(level_b - top)
    total = share_a + share_b
    mean = (share_a * own_ref[0] + share_b * other_ref[0]) / total
    level = top + jnp.log(total)
    most = jnp.max(jnp.max(jnp.abs(mean), axis=1, keepdims=True), axis=0, keepdims=True)
    ups = jnp.full((1, 1), 1.0, jnp.float32)
    downs = jnp.zeros(level.shape, jnp.float32)
    for i in range(STEPS):
        if i < STEPS - 1:
            ups = ups + jnp.where(most < 2.0 ** (3 - STEP * (i + 1)), 1.0, 0.0)
        downs = downs + jnp.where(jnp.abs(level) >= 2.0 ** (15 + STEP * i), 1.0, 0.0)
    mean = mean * scale_of(ups, STEP)
    level = level * scale_of(downs, -STEP)
    high = level.astype(jnp.bfloat16).astype(jnp.float32)
    middle = (level - high).astype(jnp.bfloat16).astype(jnp.float32)
    low = level - high - middle
    nrow = level.shape[0]
    lane = lax.broadcasted_iota(jnp.int32, level.shape, 1)
    row = lax.broadcasted_iota(jnp.int32, level.shape, 0)
    packed, counts = jnp.zeros(level.shape, jnp.float32), jnp.zeros(level.shape, jnp.float32)
    for i, part in enumerate((high, middle, low)):
        packed = jnp.where(lane == row + i * nrow, part, packed)
        counts = jnp.where(lane == row + i * nrow, downs, counts)
    packed = jnp.sum(packed, axis=0, keepdims=True)
    counts = jnp.sum(counts, axis=0, keepdims=True)
    out_ref[:nrow, :] = mean
    rest = (out_ref.shape[0] - nrow, HD)
    line = lax.broadcasted_iota(jnp.int32, rest, 0)
    out_ref[nrow:, :] = jnp.where(
        line == 0, packed, jnp.where(line == 1, counts, jnp.broadcast_to(ups, rest))
    )


def scale_of(count, step):
    scale = jnp.full(count.shape, 1.0, jnp.float32)
    for i in range(1, STEPS + 1):
        scale = jnp.where(count >= i, 2.0 ** (step * i), scale)
    return scale


def project_kernel(parts_ref, weight_ref, out_ref, rows_ref):
    ndev = parts_ref.shape[0]
    nrow = rows_ref.shape[0]
    lane = lax.broadcasted_iota(jnp.int32, (nrow, HD), 1)
    row = lax.broadcasted_iota(jnp.int32, (nrow, HD), 0)
    mine = (lane == row) | (lane == row + nrow) | (lane == row + 2 * nrow)
    levels, downs = [], []
    for d in range(ndev):
        rest = parts_ref[d, nrow:, :]
        packed = rest[0:1] * scale_of(rest[1:2], STEP)
        downs.append(scale_of(rest[2:3], -STEP))
        levels.append(jnp.sum(jnp.where(mine, packed, 0.0), axis=1, keepdims=True))
    top = functools.reduce(jnp.maximum, levels)
    total = jnp.zeros((nrow, 1), jnp.float32)
    acc = jnp.zeros((nrow, HD), jnp.float32)
    for d in range(ndev):
        share = jnp.exp(levels[d] - top)
        total = total + share
        acc = acc + share * (parts_ref[d, :nrow, :] * downs[d])
    rows_ref[...] = acc / total
    nreq = nrow // QPK
    term = jnp.zeros((nreq, weight_ref.shape[1]), jnp.float32)
    for g in range(QPK):
        heads = rows_ref[pl.ds(g, nreq, stride=QPK), :].astype(jnp.bfloat16)
        term = term + jnp.dot(
            heads, weight_ref[g * HD : (g + 1) * HD, :], preferred_element_type=jnp.float32
        )
    ndest = out_ref.shape[0]
    width = weight_ref.shape[1] // ndest
    for k in range(ndest):
        out_ref[(k - KVH_FIRST) % ndest, :, :width] = term[:, k * width : (k + 1) * width]


def planes(n, first):
    chips = [first // 2] + [i for i in range(n // 2) if i != first // 2]
    return [[2 * i + core for i in chips] for core in range(2)]


def stripes(n, firsts):
    groups = []
    for side, first in enumerate(firsts):
        chips = [first] + [i for i in range(n // 2) if i != first]
        groups.append([2 * i + (4 * i // n + side) % 2 for i in chips])
    return groups


def turned(n, first):
    return [[(first + i) % n for i in range(n)]]


def local(nctx, nkvh, hidden_in, w_query, key_cache, value_cache, chosen, owner_map, w_out):
    nreq = hidden_in.shape[0]
    nrow = nreq * QPK
    slots_here, block, _ = key_cache.shape
    params = pltpu.CompilerParams(vmem_limit_bytes=LIMIT)
    state = pltpu.VMEM((nrow, HD), jnp.float32)
    nchip = nctx // 2
    parts, items = pl.pallas_call(
        functools.partial(query_kernel, slots_here),
        out_shape=(
            jax.ShapeDtypeStruct((nrow, HD), jnp.float32),
            pltpu.SMEM((2 * SPAN + 8,), jnp.int32),
        ),
        in_specs=[HBM, HBM, HBM, HBM],
        out_specs=(VMEM, SMEM),
        scratch_shapes=[
            pltpu.VMEM(hidden_in.shape, hidden_in.dtype),
            pltpu.VMEM(w_query.shape, w_query.dtype),
            pltpu.SMEM(chosen.shape, jnp.int32),
            pltpu.SMEM(owner_map.shape, jnp.int32),
            state,
            pltpu.SemaphoreType.DMA((4,)),
        ],
        compiler_params=params,
        name="query",
    )(in_hbm(hidden_in), in_hbm(w_query), in_hbm(chosen), in_hbm(owner_map))
    swap = [(i, i ^ 1) for i in range(nctx)]
    other = lax.ppermute(parts, "ctx", swap)
    blocks = pltpu.VMEM((AHEAD, block, HD), key_cache.dtype)
    late = slots_here - AHEAD
    assert slots_here < SPAN
    keys, values = pl.pallas_call(
        fetch_kernel,
        out_shape=(blocks, blocks),
        in_specs=[SMEM, HBM, HBM],
        out_specs=(VMEM, VMEM),
        scratch_shapes=[
            pltpu.SemaphoreType.DMA((AHEAD,)),
            pltpu.SemaphoreType.DMA((AHEAD,)),
        ],
        compiler_params=params,
        cost_estimate=pl.CostEstimate(flops=0, transcendentals=0, bytes_accessed=4 << 20),
        name="fetch",
    )(items, in_hbm(key_cache), in_hbm(value_cache))
    other, keys, values = lax.optimization_barrier((other, keys, values))
    pair = ((parts + other) * QSCALE).astype(jnp.float16)
    every = jnp.broadcast_to(pair[None], (nchip, nrow, HD))
    every = lax.all_to_all(every, "ctx", 0, 0, tiled=True, axis_index_groups=stripes(nctx, STRIPE_FIRST))
    query = jnp.sum(every.astype(jnp.float32), axis=0) * (1.0 / QSCALE)
    states = pl.pallas_call(
        attend_kernel,
        out_shape=jax.ShapeDtypeStruct((2, nrow, HD), jnp.float32),
        in_specs=[VMEM, SMEM, VMEM, VMEM, HBM, HBM],
        out_specs=VMEM,
        scratch_shapes=[
            state, state, state,
            pltpu.VMEM((late, block, HD), key_cache.dtype),
            pltpu.VMEM((late, block, HD), key_cache.dtype),
            pltpu.SemaphoreType.DMA((late,)),
            pltpu.SemaphoreType.DMA((late,)),
        ],
        compiler_params=params,
        name="attend",
    )(query, items, keys, values, in_hbm(key_cache), in_hbm(value_cache))
    others = lax.ppermute(states, "ctx", swap)
    means = pl.pallas_call(
        join_kernel,
        out_shape=jax.ShapeDtypeStruct((nrow + 8, HD), jnp.float32),
        in_specs=[VMEM, VMEM],
        out_specs=VMEM,
        compiler_params=params,
        name="join",
    )(states, others)
    means = jnp.broadcast_to(means.astype(jnp.float16)[None], (nchip, *means.shape))
    means = lax.all_to_all(means, "ctx", 0, 0, tiled=True, axis_index_groups=planes(nctx, CTX_FIRST))
    means = means.astype(jnp.float32)
    terms = pl.pallas_call(
        project_kernel,
        out_shape=jax.ShapeDtypeStruct((nkvh, nreq, HD), jnp.float32),
        in_specs=[VMEM, VMEM],
        out_specs=VMEM,
        scratch_shapes=[state],
        compiler_params=params,
        name="project",
    )(means, w_out)
    terms = lax.all_to_all(terms, "kvh", 0, 0, tiled=True, axis_index_groups=turned(nkvh, KVH_FIRST))
    return jnp.sum(terms, axis=0)[:, : w_out.shape[1] // nkvh].astype(jnp.bfloat16)


def solution(mesh):
    placed = (
        P(None, "ctx"),
        P("ctx", "kvh"),
        P("ctx", None, "kvh"),
        P("ctx", None, "kvh"),
        P(None, "kvh", None),
        P(),
        P("kvh", "ctx"),
    )
    return jax.shard_map(
        functools.partial(local, mesh.shape["ctx"], mesh.shape["kvh"]),
        mesh=mesh, in_specs=placed, out_specs=P(None, ("ctx", "kvh")), check_vma=False,
    )
```
